256 devices in a mesh: req: 32 (over y, x, core), grp: 8 (over z).
Axes of the slice: x: 4, y: 4, z: 8, core: 2. Of those that a mesh axis runs over, the one named last changes fastest.
Arguments:
- queries: bfloat16 [4, 64, 8192], P(None, 'req', 'grp')
- cache_latents: bfloat16 [4, 65536, 4096], P(None, 'req', 'grp'), may hold values from -6 to 6
- fresh_latents: bfloat16 [4, 64, 4096], P(None, 'req', 'grp'), may hold values from -6 to 6
- lengths: int32 [4], replicated, may hold values from 1 to 65536, 163840 in all
- key_up: bfloat16 [8, 512, 128], P('grp'), may hold values from -0.25 to 0.25
- value_up: bfloat16 [8, 512, 128], P('grp'), may hold values from -0.25 to 0.25
- w_out: bfloat16 [8192, 8192], P('grp', 'req'), may hold values from -0.0625 to 0.0625
Outputs:
- projected: bfloat16 [256, 8192], P('grp', 'req')
The draws below stay inside these ranges and needn't reach their ends.
Inputs may be any that keep to these rules, and one draw needn't show every extreme that they name: `lengths`: each request's cached length; one request uses all 65536 positions.
All inputs are finite; a program needn't handle non-finite values.
Results may differ from the reference program's by a relative error of at most 0.019.
The reference program's roundings to bfloat16 on the way (of `latent_q` and `attention`) count: a program that leaves them out, or rounds other values in their place, can miss the bound.
Values may be sent and summed in bfloat16 or wider, within the bound.
A program may use at most 128 MiB of HBM per device.

```python
import math
import jax
import jax.numpy as jnp
import numpy as np
from jax import lax

D = 8192
GROUPS = 8
HG = 8
HD = 128
R = 512
REQS = 4
CTX_DEV = 2048
HEADS = 64
CTX = 65536
QN = 64
ROWS = 256
N_REQ = 32


def draw_queries(key, part):
    key = jax.random.fold_in(key, 7)
    values = jax.random.normal(key, (REQS, QN, HEADS * HD), jnp.float32)
    return values.astype(jnp.bfloat16)


def levels(rng, extent, cuts, least, top_value):
    factor_of, own = 1.0, jax.random.fold_in(rng, 6)
    for dim, parts in cuts:
        draws = jnp.exp(jax.random.uniform(jax.random.fold_in(own, dim), (parts,), jnp.float32, least / len(cuts), top_value / len(cuts)))
        factor_of = factor_of * jnp.repeat(draws, extent[dim] // parts).reshape([-1 if axis == dim else 1 for axis in range(len(extent))])
    return factor_of


def split_up(number_of, total, most, slope):
    portions = [(1 << 20) // math.isqrt(rank ** slope) + 1 for rank in range(2, number_of + 1)]
    spare, given = total - most - (number_of - 1), [1] * (number_of - 1)
    while spare > 0:
        movable = [i for i in range(number_of - 1) if given[i] < most]
        pool, remaining = sum([portions[i] for i in movable]), spare
        for i in movable:
            addition = min(most - given[i], max(1, remaining * portions[i] // pool), spare)
            given[i] = given[i] + addition
            spare = spare - addition
    return np.array([most] + given)


def uneven(own_key, amount, total, limit, lean):
    if amount == 2:
        one = jax.random.randint(own_key, (), max(1, total - limit), min(limit, total - 1) + 1)
        return jnp.stack([one, total - one])
    sizes = jnp.asarray(split_up(amount, total, limit, lean), jnp.int32)
    pairs = (amount - 1) // 2
    source_of, taker = sizes[1:1 + 2 * pairs:2], sizes[2:2 + 2 * pairs:2]
    slack = jnp.minimum(source_of - 1, limit - taker)
    moved = jax.random.randint(jax.random.fold_in(own_key, 1), (pairs,), 0, 1 << 20) % (slack + 1)
    sizes = sizes.at[1:1 + 2 * pairs:2].set(source_of - moved).at[2:2 + 2 * pairs:2].set(taker + moved)
    return sizes[jax.random.permutation(jax.random.fold_in(own_key, 2), amount)]


def normal_values(key, shape, scale, bound, split=(), held_as=jnp.bfloat16):
    factor_of = levels(key, shape, split, -0.22, 0.18) if split else 1.0
    values = jax.random.normal(key, shape, jnp.float32) * scale * factor_of
    return jnp.minimum(jnp.maximum(values, -bound), bound).astype(held_as)


def setup_inputs(seed: int = 0) -> dict:
    keys = jax.random.split(jax.random.key(seed), 8)
    return {
        "queries": draw_queries(jax.random.fold_in(keys[7], 71), 0),
        "cache_latents": normal_values(keys[1], (REQS, CTX, GROUPS * R), 1.0, 6.0, ((1, 32), (2, 8))),
        "fresh_latents": normal_values(keys[2], (REQS, QN, GROUPS * R), 1.0, 6.0, ((1, 32), (2, 8))),
        "lengths": uneven(keys[3], REQS, (REQS + 1) * CTX // 2, CTX, 2).astype(jnp.int32),
        "key_up": normal_values(keys[4], (GROUPS, R, HD), R ** -0.5, 0.25, ((0, 8),)),
        "value_up": normal_values(keys[5], (GROUPS, R, HD), R ** -0.5, 0.25, ((0, 8),)),
        "w_out": normal_values(keys[6], (HEADS * HD, D), (HEADS * HD) ** -0.5, 0.0625, ((0, 8), (1, 32))),
    }


NEGATIVE = -1e30


def absorb_queries(queries, key_up):
    split_rows = queries.reshape(REQS, QN, GROUPS, HG, HD).astype(jnp.float32)
    latent = jnp.einsum("righa,gca->righc", split_rows, key_up.astype(jnp.float32))
    return (latent * (HD ** -0.5)).astype(jnp.bfloat16)


def partial_block(latent_q, latents, usable):
    scores = jnp.einsum("rihc,rpc->rihp", latent_q.astype(jnp.float32), latents.astype(jnp.float32))
    usable_mask = usable[:, :, None, :]
    scores = jnp.where(usable_mask, scores, NEGATIVE)
    maxima = jnp.max(scores, axis=-1)
    weights = jnp.where(usable_mask, jnp.exp(scores - maxima[..., None]), 0.0)
    sums_exp = jnp.sum(weights, axis=-1)
    weighted = jnp.einsum("rihp,rpc->rihc", weights.astype(jnp.bfloat16).astype(jnp.float32), latents.astype(jnp.float32))
    return maxima, sums_exp, weighted


def reference(queries, cache_latents, fresh_latents, lengths, key_up, value_up, w_out):
    latent_q = absorb_queries(queries, key_up)
    blocks = cache_latents.reshape(REQS, N_REQ, CTX_DEV, GROUPS, R)
    row_ids = jnp.arange(QN, dtype=jnp.int32)
    fresh_usable = jnp.broadcast_to(row_ids[None, :] <= row_ids[:, None], (REQS, QN, QN))
    outputs = []
    for group_idx in range(GROUPS):
        group_query = latent_q[:, :, group_idx]

        def one_block(block_idx):
            block_all = lax.dynamic_index_in_dim(blocks, block_idx, 1, keepdims=False)
            group_cache = block_all[:, :, group_idx]
            positions = block_idx * CTX_DEV + jnp.arange(CTX_DEV, dtype=jnp.int32)
            usable = jnp.broadcast_to(positions[None, None, :] < lengths[:, None, None], (REQS, QN, CTX_DEV))
            return partial_block(group_query, group_cache, usable)

        maxima, sums_exp, weighted = lax.map(one_block, jnp.arange(N_REQ, dtype=jnp.int32))
        fresh_group = fresh_latents[:, :, group_idx * R:(group_idx + 1) * R]
        fresh_max, fresh_sums, fresh_weighted = partial_block(group_query, fresh_group, fresh_usable)
        highest = jnp.maximum(jnp.max(maxima, axis=0), fresh_max)
        block_scale = jnp.exp(maxima - highest)
        fresh_scale = jnp.exp(fresh_max - highest)
        total = jnp.sum(block_scale * sums_exp, axis=0) + fresh_scale * fresh_sums
        combined = jnp.sum(block_scale[..., None] * weighted, axis=0) + fresh_scale[..., None] * fresh_weighted
        latent_out = combined / total[..., None]
        head_out = jnp.einsum("rihc,ca->riha", latent_out, value_up[group_idx].astype(jnp.float32), precision=lax.Precision.HIGHEST)
        outputs.append(head_out.astype(jnp.bfloat16))
    attention = jnp.stack(outputs, axis=2).reshape(ROWS, HEADS * HD)
    return jnp.dot(attention, w_out, preferred_element_type=jnp.float32).astype(jnp.bfloat16)
```

```python
import functools

import jax
import jax.numpy as jnp
from jax import lax
from jax.experimental import pallas as pl
from jax.experimental.pallas import tpu as pltpu
from jax.sharding import PartitionSpec as P

MESH = pl.DeviceIdType.MESH
NEGATIVE = -1e30

REQS = 4
PEERS = 32
GRPS = 8
HG = 8
HD = 128
RANK = 512
QN = 64
ROWS = QN * HG
EXTENT = 2048
OWN = ROWS // PEERS
CHUNK = 256
WIDE = 256


def dot_nt(a, b):
    return lax.dot_general(a, b, (((1,), (1,)), ((), ())), preferred_element_type=jnp.float32)


def dot_nn(a, b):
    return jnp.dot(a, b, preferred_element_type=jnp.float32)


def stat_rows(maxima, sums):
    n = maxima.shape[0] // OWN
    shape = (maxima.shape[0], 128)
    lane = lax.broadcasted_iota(jnp.int32, shape, 1)
    row = lax.rem(lax.broadcasted_iota(jnp.int32, shape, 0), OWN)
    spread = jnp.where(lane == row, maxima, jnp.where(lane == row + OWN, sums, 0.0))
    return jnp.sum(spread.reshape(n, OWN, 128), axis=1)


def kernel(
    len_ref, q_ref, f_ref, cache, ku_hbm, vu_hbm, wo_hbm, out_ref,
    held, ku, vu, wo,
    q_rows, q_send, q_all, q_wide, q_perm,
    f_rows, f_send, f_all, f_wide, f_keys,
    latent, o_send, o_all, s_send, s_all, f_out, f_stat,
    a_send, a_all, y_send, y_all,
    held_sem, w_sem, q_ssem, q_rsem, f_ssem, f_rsem, o_ssem, o_rsem, s_ssem, s_rsem,
    a_ssem, a_rsem, y_ssem, y_rsem,
):
    me = lax.axis_index("req")
    grp = lax.axis_index("grp")

    barrier = pltpu.get_barrier_semaphore()

    @pl.loop(1, PEERS)
    def _(j):
        pl.semaphore_signal(barrier, inc=1, device_id=(lax.rem(me + j, PEERS), grp), device_id_type=MESH)

    @pl.loop(1, GRPS)
    def _(j):
        pl.semaphore_signal(barrier, inc=1, device_id=(me, lax.rem(grp + j, GRPS)), device_id_type=MESH)

    def fetch_weights(i):
        return pltpu.make_async_copy((ku_hbm, vu_hbm, wo_hbm)[i], (ku, vu, wo)[i], w_sem.at[i])

    def fetch_cache(r):
        return pltpu.make_async_copy(cache.at[r], held.at[r], held_sem.at[r])

    fetch_weights(0).start()

    @pl.loop(0, REQS)
    def _(r):
        fetch_cache(r).start()

    fetch_weights(1).start()
    fetch_weights(2).start()

    for r in range(REQS):
        wide = q_ref[r].astype(jnp.float32)
        for i in range(2):
            for h in range(HG):
                q_rows[pl.ds(r * OWN + i * HG + h, 1), :] = wide[i:i + 1, h * HD:(h + 1) * HD]
        fresh = f_ref[r].astype(jnp.float32)
        for i in range(2):
            for c in range(4):
                f_rows[pl.ds(i * 16 + r * 4 + c, 1), :] = fresh[i:i + 1, c * 128:(c + 1) * 128]
    q_send[...] = q_rows[...].astype(jnp.bfloat16).reshape(REQS, OWN, HD)
    f_send[...] = f_rows[...].astype(jnp.bfloat16)

    pl.semaphore_wait(barrier, PEERS - 1 + GRPS - 1)

    def send_all(src, dst, send_sem, recv_sem):
        @pl.loop(0, PEERS - 1)
        def _(j):
            peer = lax.rem(me + 1 + lax.rem(j + 16, PEERS - 1), PEERS)
            pltpu.make_async_remote_copy(
                src_ref=src, dst_ref=dst, send_sem=send_sem, recv_sem=recv_sem,
                device_id=(peer, grp), device_id_type=MESH,
            ).start()
        pltpu.make_async_copy(src, dst, recv_sem).start()

    @pl.loop(0, REQS)
    def _(r):
        send_all(q_send.at[r], q_all.at[r, me], q_ssem.at[r], q_rsem.at[r])

    send_all(f_send, f_all.at[me], f_ssem, f_rsem)
    fetch_weights(0).wait()
    fetch_weights(1).wait()

    @pl.loop(0, REQS)
    def _(r):
        pltpu.make_async_copy(q_all.at[r], q_all.at[r], q_rsem.at[r]).wait()
        q_wide[...] = q_all[r].reshape(ROWS, HD).astype(jnp.float32)
        for h in range(HG):
            q_perm[h * QN:(h + 1) * QN, :] = q_wide[pl.ds(h, QN, stride=HG), :].astype(jnp.bfloat16)
        latent[r] = (dot_nt(q_perm[...], ku[...]) * HD ** (-0.5)).astype(jnp.bfloat16)
        fetch_cache(r).wait()
        position = me * EXTENT + lax.broadcasted_iota(jnp.int32, (1, EXTENT), 1)
        bias = jnp.where(position < len_ref[r], 0.0, -jnp.inf)
        for c in range(ROWS // CHUNK):
            rows = slice(c * CHUNK, (c + 1) * CHUNK)
            scores = dot_nt(latent[r, rows, :], held[r]) + bias
            maxima = jnp.maximum(jnp.max(scores, axis=1, keepdims=True), NEGATIVE)
            weights = jnp.exp(scores - maxima)
            sums = jnp.sum(weights, axis=1, keepdims=True)
            weighted = dot_nn(weights.astype(jnp.bfloat16), held[r])
            headed = dot_nn(weighted.astype(jnp.bfloat16), vu[...])
            owners = slice(c * CHUNK // OWN, (c + 1) * CHUNK // OWN)
            o_send[r, owners] = headed.astype(jnp.bfloat16).reshape(CHUNK // OWN, OWN, HD)
            s_send[r, owners, 0, :] = stat_rows(maxima, sums)

        @pl.loop(0, PEERS - 1)
        def _(j):
            peer = lax.rem(me + 1 + lax.rem(j + 16, PEERS - 1), PEERS)
            pltpu.make_async_remote_copy(
                src_ref=o_send.at[r, peer], dst_ref=o_all.at[r, me], send_sem=o_ssem.at[r], recv_sem=o_rsem.at[r],
                device_id=(peer, grp), device_id_type=MESH,
            ).start()
            pltpu.make_async_remote_copy(
                src_ref=s_send.at[r, peer], dst_ref=s_all.at[r, me], send_sem=s_ssem.at[r], recv_sem=s_rsem.at[r],
                device_id=(peer, grp), device_id_type=MESH,
            ).start()
        pltpu.make_async_copy(o_send.at[r, me], o_all.at[r, me], o_rsem.at[r]).start()
        pltpu.make_async_copy(s_send.at[r, me], s_all.at[r, me], s_rsem.at[r]).start()

    pltpu.make_async_copy(f_all, f_all, f_rsem).wait()
    f_wide[...] = f_all[...].astype(jnp.float32).reshape(QN * 16, 128)
    first = lax.rem(me, QN // OWN) * OWN

    @pl.loop(0, REQS)
    def _(r):
        for c in range(4):
            f_keys[:, c * 128:(c + 1) * 128] = f_wide[pl.ds(r * 4 + c, QN, stride=16), :].astype(jnp.bfloat16)
        own = latent[r, pl.ds(pl.multiple_of(me * OWN, OWN), OWN), :]
        scores = dot_nt(own, f_keys[...])
        row = first + lax.broadcasted_iota(jnp.int32, (OWN, QN), 0)
        usable = lax.broadcasted_iota(jnp.int32, (OWN, QN), 1) <= row
        scores = jnp.where(usable, scores, NEGATIVE)
        maxima = jnp.max(scores, axis=1, keepdims=True)
        weights = jnp.where(usable, jnp.exp(scores - maxima), 0.0)
        sums = jnp.sum(weights, axis=1, keepdims=True)
        weighted = dot_nn(weights.astype(jnp.bfloat16), f_keys[...])
        f_out[r] = dot_nn(weighted.astype(jnp.bfloat16), vu[...])
        f_stat[r] = stat_rows(maxima, sums)

    diagonal = lax.broadcasted_iota(jnp.int32, (OWN, 128), 0) == lax.broadcasted_iota(jnp.int32, (OWN, 128), 1)
    head_at = pl.ds(pl.multiple_of(me // (QN // OWN) * HD, HD), HD)
    row_at = pl.ds(pl.multiple_of(first, OWN), OWN)

    @pl.loop(0, REQS)
    def _(r):
        pltpu.make_async_copy(s_all.at[r], s_all.at[r], s_rsem.at[r]).wait()
        stats = s_all[r, :, 0, :]
        own_stat = f_stat[r]
        highest = jnp.maximum(jnp.max(stats, axis=0, keepdims=True), own_stat)
        scale = jnp.exp(stats - highest)
        own_scale = jnp.exp(own_stat - highest)
        total = jnp.sum(scale * pltpu.roll(stats, 128 - OWN, 1), axis=0, keepdims=True)
        total = total + own_scale * pltpu.roll(jnp.broadcast_to(own_stat, (8, 128)), 128 - OWN, 1)[:1]
        share = scale / total
        own_share = own_scale / total
        column = jnp.sum(jnp.where(diagonal[None], share[:, None, :], 0.0), axis=2, keepdims=True)
        own_column = jnp.sum(jnp.where(diagonal, own_share, 0.0), axis=1, keepdims=True)
        pltpu.make_async_copy(o_all.at[r], o_all.at[r], o_rsem.at[r]).wait()
        heads = jnp.sum(column * o_all[r].astype(jnp.float32), axis=0) + own_column * f_out[r]
        a_send[r] = heads.astype(jnp.bfloat16)
        send_all(a_send.at[r], a_all.at[r, row_at, head_at], a_ssem.at[r], a_rsem.at[r])

    fetch_weights(2).wait()

    @pl.loop(0, REQS)
    def _(r):
        pltpu.make_async_copy(a_all.at[r], a_all.at[r], a_rsem.at[r]).wait()
        y_send[r] = dot_nn(a_all[r], wo[...]).astype(jnp.bfloat16).reshape(2, QN // 2, WIDE)
        for half in range(2):
            @pl.when(r * 2 + half != grp)
            def _():
                pltpu.make_async_remote_copy(
                    src_ref=y_send.at[r, half], dst_ref=y_all.at[grp], send_sem=y_ssem, recv_sem=y_rsem,
                    device_id=(me, r * 2 + half), device_id_type=MESH,
                ).start()

            @pl.when(r * 2 + half == grp)
            def _():
                pltpu.make_async_copy(y_send.at[r, half], y_all.at[grp], y_rsem).start()

    pltpu.make_async_copy(y_all, y_all, y_rsem).wait()
    out_ref[...] = jnp.sum(y_all[...].astype(jnp.float32), axis=0).astype(jnp.bfloat16)

    others = pl.ds(0, PEERS - 1)

    @pl.loop(0, REQS)
    def _(r):
        for buffer, sem in ((q_all, q_ssem), (o_all, o_ssem), (s_all, s_ssem), (q_all, a_ssem)):
            pltpu.make_async_copy(buffer.at[r, others], buffer.at[r, others], sem.at[r]).wait()

    pltpu.make_async_copy(f_all.at[others], f_all.at[others], f_ssem).wait()
    pltpu.make_async_copy(y_all.at[pl.ds(0, GRPS - 1)], y_all.at[pl.ds(0, GRPS - 1)], y_ssem).wait()


def on_device(lengths, queries, fresh_latents, cache_latents, key_up, value_up, w_out):
    bf16, f32 = jnp.bfloat16, jnp.float32
    any_space = pl.BlockSpec(memory_space=pl.ANY)
    vmem = pl.BlockSpec(memory_space=pltpu.VMEM)
    dma, dmas = pltpu.SemaphoreType.DMA, pltpu.SemaphoreType.DMA((REQS,))
    return pl.pallas_call(
        kernel,
        out_shape=jax.ShapeDtypeStruct((QN * REQS // GRPS, WIDE), bf16),
        in_specs=[pl.BlockSpec(memory_space=pltpu.SMEM), vmem, vmem] + [any_space] * 4,
        out_specs=vmem,
        scratch_shapes=[
            pltpu.VMEM((REQS, EXTENT, RANK), bf16),
            pltpu.VMEM((RANK, HD), bf16),
            pltpu.VMEM((RANK, HD), bf16),
            pltpu.VMEM((HG * HD, WIDE), bf16),
            pltpu.VMEM((REQS * OWN, HD), f32),
            pltpu.VMEM((REQS, OWN, HD), bf16),
            pltpu.VMEM((REQS, PEERS, OWN, HD), bf16),
            pltpu.VMEM((ROWS, HD), f32),
            pltpu.VMEM((ROWS, HD), bf16),
            pltpu.VMEM((REQS * 8, 128), f32),
            pltpu.VMEM((REQS * 8, 128), bf16),
            pltpu.VMEM((PEERS, REQS * 8, 128), bf16),
            pltpu.VMEM((QN * 16, 128), f32),
            pltpu.VMEM((QN, RANK), bf16),
            pltpu.VMEM((REQS, ROWS, RANK), bf16),
            pltpu.VMEM((REQS, PEERS, OWN, HD), bf16),
            pltpu.VMEM((REQS, PEERS, OWN, HD), bf16),
            pltpu.VMEM((REQS, PEERS, 1, 128), f32),
            pltpu.VMEM((REQS, PEERS, 1, 128), f32),
            pltpu.VMEM((REQS, OWN, HD), f32),
            pltpu.VMEM((REQS, 1, 128), f32),
            pltpu.VMEM((REQS, OWN, HD), bf16),
            pltpu.VMEM((REQS, QN, HG * HD), bf16),
            pltpu.VMEM((REQS, 2, QN // 2, WIDE), bf16),
            pltpu.VMEM((GRPS, QN // 2, WIDE), bf16),
            dmas, pltpu.SemaphoreType.DMA((3,)), dmas, dmas, dma, dma, dmas, dmas, dmas, dmas,
            dmas, dmas, dma, dma,
        ],
        compiler_params=pltpu.CompilerParams(
            collective_id=0, has_side_effects=True, vmem_limit_bytes=56 * 2 ** 20
        ),
    )(lengths, queries, fresh_latents, cache_latents, key_up, value_up, w_out)


def solution(mesh):
    def whole(queries, cache_latents, fresh_latents, lengths, key_up, value_up, w_out):
        return jax.shard_map(
            lambda q, c, f, n, k, v, w: on_device(
                n, q, f, c, k.reshape(RANK, HD), v.reshape(RANK, HD), w
            ),
            mesh=mesh,
            in_specs=(
                P(None, "req", "grp"),
                P(None, "req", "grp"),
                P(None, "req", "grp"),
                P(),
                P("grp", None, None),
                P("grp", None, None),
                P("grp", "req"),
            ),
            out_specs=P("grp", "req"),
            check_vma=False,
        )(queries, cache_latents, fresh_latents, lengths, key_up, value_up, w_out)

    return whole
```

```python
import functools

import jax
import jax.numpy as jnp
from jax import lax
from jax.experimental import pallas as pl
from jax.experimental.pallas import tpu as pltpu
from jax.sharding import PartitionSpec as P

MESH = pl.DeviceIdType.MESH
NEGATIVE = -1e30

REQS = 4
PEERS = 32
GRPS = 8
HG = 8
HD = 128
RANK = 512
QN = 64
ROWS = QN * HG
EXTENT = 2048
OWN = ROWS // PEERS
CHUNK = 256
BLOCK = 1024
CHIPS = PEERS // 2
WIDE = 256


def dot_nt(a, b):
    return lax.dot_general(a, b, (((1,), (1,)), ((), ())), preferred_element_type=jnp.float32)


def dot_nn(a, b):
    return jnp.dot(a, b, preferred_element_type=jnp.float32)


def stat_rows(maxima, sums):
    n = maxima.shape[0] // OWN
    lane = lax.broadcasted_iota(jnp.int32, (OWN, 128), 1)
    row = lax.broadcasted_iota(jnp.int32, (OWN, 128), 0)
    sums = jnp.where((lane == row + OWN)[None], sums.reshape(n, OWN, 1), 0.0)
    return jnp.sum(jnp.where((lane == row)[None], maxima.reshape(n, OWN, 1), sums), axis=1)


def attend(queries, keys, bias):
    chunks, blocks = ROWS // CHUNK, EXTENT // BLOCK
    items = [(b, c) for b in range(blocks) for c in range(chunks)]

    def score(b, c):
        at = slice(b * BLOCK, (b + 1) * BLOCK)
        return dot_nt(queries[c * CHUNK:(c + 1) * CHUNK, :], keys[at, :]) + bias[:, at]

    parts = [None] * chunks
    ahead = score(*items[0])
    for k, (b, c) in enumerate(items):
        scores = ahead
        if k + 1 < len(items):
            ahead = score(*items[k + 1])
        maxima = jnp.maximum(jnp.max(scores, axis=1, keepdims=True), NEGATIVE)
        if parts[c] is not None:
            maxima = jnp.maximum(maxima, parts[c][0])
        weights = jnp.exp(scores - maxima)
        sums = jnp.sum(weights, axis=1, keepdims=True)
        weighted = dot_nn(weights.astype(jnp.bfloat16), keys[b * BLOCK:(b + 1) * BLOCK, :])
        if parts[c] is not None:
            scale = jnp.exp(parts[c][0] - maxima)
            sums = sums + scale * parts[c][1]
            weighted = weighted + scale * parts[c][2]
        parts[c] = (maxima, sums, weighted)
    return parts


def kernel(
    len_hbm, q_hbm, f_hbm, cache, ku_hbm, vu_hbm, wo_hbm, out_ref,
    len_ref, q_ref, f_ref, held, ku, vu, wo,
    q_rows, q_send, q_all, q_wide, q_perm,
    f_rows, f_send, f_all, f_wide, f_keys,
    latent, o_send, o_all, s_send, s_all, f_out, f_stat,
    a_send, a_all, y_send, y_all,
    held_sem, w_sem, q_ssem, q_rsem, f_ssem, f_rsem, o_ssem, o_rsem, s_ssem, s_rsem,
    a_ssem, a_rsem, y_ssem, y_rsem, p_ssem,
):
    me = lax.axis_index("req")
    grp = lax.axis_index("grp")
    chip, core = me // 2, lax.rem(me, 2)
    sibling = me + 1 - 2 * core
    def owned(peer):
        return peer // 4 * 4 + lax.rem(peer, 2) * 2 + lax.rem(peer // 2, 2)

    mine = owned(me)

    barrier = pltpu.get_barrier_semaphore()

    @pl.loop(1, PEERS, unroll=True)
    def _(j):
        pl.semaphore_signal(barrier, inc=1, device_id=(lax.rem(me + j, PEERS), grp), device_id_type=MESH)

    @pl.loop(1, GRPS, unroll=True)
    def _(j):
        pl.semaphore_signal(barrier, inc=1, device_id=(me, lax.rem(grp + j, GRPS)), device_id_type=MESH)

    def fetch_weights(i):
        sources, targets = (ku_hbm, vu_hbm, wo_hbm, q_hbm, f_hbm, len_hbm), (ku, vu, wo, q_ref, f_ref, len_ref)
        return pltpu.make_async_copy(sources[i], targets[i], w_sem.at[i])

    def fetch_cache(r):
        return pltpu.make_async_copy(cache.at[r], held.at[r], held_sem.at[r])

    for i in (3, 4, 5, 0, 1):
        fetch_weights(i).start()

    @pl.loop(0, REQS)
    def _(r):
        fetch_cache(r).start()

    fetch_weights(2).start()
    for i in (3, 4, 5):
        fetch_weights(i).wait()

    for r in range(REQS):
        wide = q_ref[r].astype(jnp.float32)
        for i in range(2):
            for h in range(HG):
                q_rows[pl.ds(r * OWN + i * HG + h, 1), :] = wide[i:i + 1, h * HD:(h + 1) * HD]
        fresh = f_ref[r].astype(jnp.float32)
        for i in range(2):
            for c in range(4):
                f_rows[pl.ds(i * 16 + r * 4 + c, 1), :] = fresh[i:i + 1, c * 128:(c + 1) * 128]
    q_send[...] = q_rows[...].astype(jnp.bfloat16).reshape(REQS, OWN, HD)
    f_send[...] = f_rows[...].astype(jnp.bfloat16)

    pl.semaphore_wait(barrier, PEERS - 1 + GRPS - 1)

    def remote(src, dst, send_sem, recv_sem, peer):
        return pltpu.make_async_remote_copy(
            src_ref=src, dst_ref=dst, send_sem=send_sem, recv_sem=recv_sem,
            device_id=(peer, grp), device_id_type=MESH,
        )

    def send_all(src, dst, send_sem, recv_sem):
        @pl.loop(0, PEERS - 1, unroll=True)
        def _(j):
            remote(src, dst, send_sem, recv_sem, lax.rem(me + 1 + lax.rem(j + 16, PEERS - 1), PEERS)).start()
        pltpu.make_async_copy(src, dst, recv_sem).start()

    def send_chips(src, dst, send_sem, recv_sem):
        @pl.loop(0, CHIPS - 1, unroll=True)
        def _(j):
            remote(src, dst, send_sem, recv_sem, lax.rem(me + 2 + 2 * lax.rem(j + 7, CHIPS - 1), PEERS)).start()
        pltpu.make_async_copy(src, dst, recv_sem).start()

    def pass_on(buffer, send_sem, recv_sem):
        pltpu.make_async_copy(buffer, buffer, recv_sem).wait()
        remote(buffer, buffer, send_sem, recv_sem, sibling).start()

    def await_all(buffer, sem):
        pltpu.make_async_copy(buffer, buffer, sem).wait()

    send_all(q_send.at[0], q_all.at[0, core, chip], q_ssem.at[0], q_rsem.at[0, core])

    @pl.loop(1, REQS)
    def _(r):
        send_chips(q_send.at[r], q_all.at[r, core, chip], q_ssem.at[r], q_rsem.at[r, core])

    fetch_weights(0).wait()
    fetch_weights(1).wait()
    await_all(q_all.at[0, core], q_rsem.at[0, core])

    @pl.loop(0, REQS)
    def _(r):
        await_all(q_all.at[r, 1 - core], q_rsem.at[r, 1 - core])
        for d in range(PEERS):
            q_wide[d * OWN:(d + 1) * OWN, :] = q_all[r, d % 2, d // 2].astype(jnp.float32)
        for h in range(HG):
            q_perm[h * QN:(h + 1) * QN, :] = q_wide[pl.ds(h, QN, stride=HG), :].astype(jnp.bfloat16)
        latent[r] = (dot_nt(q_perm[...], ku[...]) * HD ** (-0.5)).astype(jnp.bfloat16)

        @pl.when(r < REQS - 1)
        def _():
            pass_on(q_all.at[r + 1, core], p_ssem.at[0, r], q_rsem.at[r + 1, core])

        @pl.when(r == 0)
        def _():
            send_chips(f_send, f_all.at[core, chip], f_ssem, f_rsem.at[core])

        fetch_cache(r).wait()
        position = me * EXTENT + lax.broadcasted_iota(jnp.int32, (1, EXTENT), 1)
        bias = jnp.where(position < len_ref[r], 0.0, -jnp.inf)
        for c, (maxima, sums, weighted) in enumerate(attend(latent.at[r], held.at[r], bias)):
            headed = dot_nn(weighted.astype(jnp.bfloat16), vu[...])
            owners = slice(c * CHUNK // OWN, (c + 1) * CHUNK // OWN)
            o_send[r, owners] = headed.astype(jnp.bfloat16).reshape(CHUNK // OWN, OWN, HD)
            s_send[r, owners, 0, :] = stat_rows(maxima, sums)

        @pl.loop(0, PEERS - 1, unroll=True)
        def _(j):
            peer = lax.rem(me + 1 + lax.rem(j + 16, PEERS - 1), PEERS)
            block = owned(peer)
            remote(o_send.at[r, block], o_all.at[r, me], o_ssem.at[r], o_rsem.at[r], peer).start()
            remote(s_send.at[r, block], s_all.at[r, me], s_ssem.at[r], s_rsem.at[r], peer).start()
        pltpu.make_async_copy(o_send.at[r, mine], o_all.at[r, me], o_rsem.at[r]).start()
        pltpu.make_async_copy(s_send.at[r, mine], s_all.at[r, me], s_rsem.at[r]).start()

    pass_on(f_all.at[core], p_ssem.at[0, REQS - 1], f_rsem.at[core])
    await_all(f_all.at[1 - core], f_rsem.at[1 - core])
    for d in range(PEERS):
        f_wide[d * 32:(d + 1) * 32, :] = f_all[d % 2, d // 2].astype(jnp.float32)
    first = (core * 2 + lax.rem(chip, 2)) * OWN

    @pl.loop(0, REQS)
    def _(r):
        for c in range(4):
            f_keys[:, c * 128:(c + 1) * 128] = f_wide[pl.ds(r * 4 + c, QN, stride=16), :].astype(jnp.bfloat16)
        own = latent[r, pl.ds(pl.multiple_of(mine * OWN, OWN), OWN), :]
        scores = dot_nt(own, f_keys[...])
        row = first + lax.broadcasted_iota(jnp.int32, (OWN, QN), 0)
        usable = lax.broadcasted_iota(jnp.int32, (OWN, QN), 1) <= row
        scores = jnp.where(usable, scores, NEGATIVE)
        maxima = jnp.max(scores, axis=1, keepdims=True)
        weights = jnp.where(usable, jnp.exp(scores - maxima), 0.0)
        sums = jnp.sum(weights, axis=1, keepdims=True)
        weighted = dot_nn(weights.astype(jnp.bfloat16), f_keys[...])
        f_out[r] = dot_nn(weighted.astype(jnp.bfloat16), vu[...])
        f_stat[r] = stat_rows(maxima, sums)

    diagonal = lax.broadcasted_iota(jnp.int32, (OWN, 128), 0) == lax.broadcasted_iota(jnp.int32, (OWN, 128), 1)
    head_at = pl.ds(pl.multiple_of(chip // 2 * HD, HD), HD)
    row_at = pl.ds(pl.multiple_of(lax.rem(chip, 2) * OWN, OWN), OWN)

    @pl.loop(0, REQS)
    def _(r):
        pltpu.make_async_copy(s_all.at[r], s_all.at[r], s_rsem.at[r]).wait()
        stats = s_all[r, :, 0, :]
        own_stat = f_stat[r]
        highest = jnp.maximum(jnp.max(stats, axis=0, keepdims=True), own_stat)
        scale = jnp.exp(stats - highest)
        own_scale = jnp.exp(own_stat - highest)
        total = jnp.sum(scale * pltpu.roll(stats, 128 - OWN, 1), axis=0, keepdims=True)
        total = total + own_scale * pltpu.roll(jnp.broadcast_to(own_stat, (8, 128)), 128 - OWN, 1)[:1]
        share = scale / total
        own_share = own_scale / total
        column = jnp.sum(jnp.where(diagonal[None], share[:, None, :], 0.0), axis=2, keepdims=True)
        own_column = jnp.sum(jnp.where(diagonal, own_share, 0.0), axis=1, keepdims=True)
        pltpu.make_async_copy(o_all.at[r], o_all.at[r], o_rsem.at[r]).wait()
        heads = jnp.sum(column * o_all[r].astype(jnp.float32), axis=0) + own_column * f_out[r]
        a_send[r] = heads.astype(jnp.bfloat16)
        own_block = a_all.at[r, core, row_at, head_at]

        @pl.when(r < REQS - 1)
        def _():
            send_chips(a_send.at[r], own_block, a_ssem.at[r], a_rsem.at[r, core])

        @pl.when(r == REQS - 1)
        def _():
            send_all(a_send.at[r], own_block, a_ssem.at[r], a_rsem.at[r, core])

    @pl.loop(0, REQS - 1)
    def _(r):
        pass_on(a_all.at[r, core], p_ssem.at[1, r], a_rsem.at[r, core])

    fetch_weights(2).wait()

    @pl.loop(0, REQS)
    def _(r):
        @pl.when(r == REQS - 1)
        def _():
            await_all(a_all.at[r, core], a_rsem.at[r, core])

        await_all(a_all.at[r, 1 - core], a_rsem.at[r, 1 - core])
        product = dot_nn(a_all[r].reshape(QN, HG * HD), wo[...])
        y_send[r] = product.astype(jnp.bfloat16).reshape(2, QN // 2, WIDE)
        for half in range(2):
            @pl.when(r * 2 + half != grp)
            def _():
                pltpu.make_async_remote_copy(
                    src_ref=y_send.at[r, half], dst_ref=y_all.at[grp], send_sem=y_ssem, recv_sem=y_rsem,
                    device_id=(me, r * 2 + half), device_id_type=MESH,
                ).start()

            @pl.when(r * 2 + half == grp)
            def _():
                pltpu.make_async_copy(y_send.at[r, half], y_all.at[grp], y_rsem).start()

    others = pl.ds(0, PEERS - 1)
    chips = pl.ds(0, CHIPS - 1)

    @pl.loop(0, REQS)
    def _(r):
        await_all(o_all.at[r, others], o_ssem.at[r])
        await_all(s_all.at[r, others], s_ssem.at[r])

    await_all(o_all.at[0, others], q_ssem.at[0])
    await_all(o_all.at[0, others], a_ssem.at[REQS - 1])

    @pl.loop(0, REQS - 1)
    def _(r):
        await_all(q_all.at[0, 0, chips], q_ssem.at[r + 1])
        await_all(q_all.at[0, 0], p_ssem.at[0, r])
        await_all(q_all.at[0, 0, chips], a_ssem.at[r])
        await_all(q_all.at[0, 0], p_ssem.at[1, r])

    await_all(f_all.at[0, chips], f_ssem)
    await_all(f_all.at[0], p_ssem.at[0, REQS - 1])
    pltpu.make_async_copy(y_all, y_all, y_rsem).wait()
    out_ref[...] = jnp.sum(y_all[...].astype(jnp.float32), axis=0).astype(jnp.bfloat16)
    await_all(y_all.at[pl.ds(0, GRPS - 1)], y_ssem)


def on_device(lengths, queries, fresh_latents, cache_latents, key_up, value_up, w_out):
    bf16, f32 = jnp.bfloat16, jnp.float32
    any_space = pl.BlockSpec(memory_space=pl.ANY)
    vmem = pl.BlockSpec(memory_space=pltpu.VMEM)
    dma, dmas = pltpu.SemaphoreType.DMA, pltpu.SemaphoreType.DMA((REQS,))
    pairs = pltpu.SemaphoreType.DMA((REQS, 2))
    return pl.pallas_call(
        kernel,
        out_shape=jax.ShapeDtypeStruct((QN * REQS // GRPS, WIDE), bf16),
        in_specs=[any_space] * 7,
        out_specs=vmem,
        scratch_shapes=[
            pltpu.SMEM((REQS,), jnp.int32),
            pltpu.VMEM((REQS, 2, HG * HD), bf16),
            pltpu.VMEM((REQS, 2, RANK), bf16),
            pltpu.VMEM((REQS, EXTENT, RANK), bf16),
            pltpu.VMEM((RANK, HD), bf16),
            pltpu.VMEM((RANK, HD), bf16),
            pltpu.VMEM((HG * HD, WIDE), bf16),
            pltpu.VMEM((REQS * OWN, HD), f32),
            pltpu.VMEM((REQS, OWN, HD), bf16),
            pltpu.VMEM((REQS, 2, CHIPS, OWN, HD), bf16),
            pltpu.VMEM((ROWS, HD), f32),
            pltpu.VMEM((ROWS, HD), bf16),
            pltpu.VMEM((REQS * 8, 128), f32),
            pltpu.VMEM((REQS * 8, 128), bf16),
            pltpu.VMEM((2, CHIPS, REQS * 8, 128), bf16),
            pltpu.VMEM((QN * 16, 128), f32),
            pltpu.VMEM((QN, RANK), bf16),
            pltpu.VMEM((REQS, ROWS, RANK), bf16),
            pltpu.VMEM((REQS, PEERS, OWN, HD), bf16),
            pltpu.VMEM((REQS, PEERS, OWN, HD), bf16),
            pltpu.VMEM((REQS, PEERS, 1, 128), f32),
            pltpu.VMEM((REQS, PEERS, 1, 128), f32),
            pltpu.VMEM((REQS, OWN, HD), f32),
            pltpu.VMEM((REQS, 1, 128), f32),
            pltpu.VMEM((REQS, OWN, HD), bf16),
            pltpu.VMEM((REQS, 2, QN // 2, HG * HD), bf16),
            pltpu.VMEM((REQS, 2, QN // 2, WIDE), bf16),
            pltpu.VMEM((GRPS, QN // 2, WIDE), bf16),
            dmas, pltpu.SemaphoreType.DMA((6,)), dmas, pairs, dma, pltpu.SemaphoreType.DMA((2,)),
            dmas, dmas, dmas, dmas, dmas, pairs, dma, dma, pltpu.SemaphoreType.DMA((2, REQS)),
        ],
        compiler_params=pltpu.CompilerParams(
            collective_id=0, has_side_effects=True, vmem_limit_bytes=56 * 2 ** 20
        ),
    )(lengths, queries, fresh_latents, cache_latents, key_up, value_up, w_out)


def solution(mesh):
    def whole(queries, cache_latents, fresh_latents, lengths, key_up, value_up, w_out):
        return jax.shard_map(
            lambda q, c, f, n, k, v, w: on_device(
                n, q, f, c, k.reshape(RANK, HD), v.reshape(RANK, HD), w
            ),
            mesh=mesh,
            in_specs=(
                P(None, "req", "grp"),
                P(None, "req", "grp"),
                P(None, "req", "grp"),
                P(),
                P("grp", None, None),
                P("grp", None, None),
                P("grp", "req"),
            ),
            out_specs=P("grp", "req"),
            check_vma=False,
        )(queries, cache_latents, fresh_latents, lengths, key_up, value_up, w_out)

    return whole
```
